512 devices in a mesh: row: 64 (over z, x, core), grp: 8 (over y).
Axes of the slice: x: 4, y: 8, z: 8, core: 2. Of those that a mesh axis runs over, the one named last changes fastest.
Arguments:
- panel_rows: bfloat16 [262144, 1024], P(('row', 'grp')), may hold values from -300 to 300, as said below
- sign_bits: int32 [262144], P(('row', 'grp')), may hold values from 0 to 1
- sample_rows: int32 [8192], replicated, may hold values from 0 to 262143, as said below
Outputs:
- factor: float32 [1024, 1024], P('row', 'grp')
The draws below stay inside these ranges and needn't reach their ends.
Inputs may be any that keep to these rules, and one draw needn't show every extreme that they name: `sample_rows`: distinct and ascending. Each aligned block of 512 rows (the rows of one device) holds at most 32 sampled rows, and at least a quarter of these blocks hold exactly 32. `panel_rows`: finite values.
All inputs are finite; a program needn't handle non-finite values.
Results may differ from the reference program's by a relative error of at most 0.0011.
Values may be sent and summed in bfloat16 or wider, within the bound.
A program may use at most 64 MiB of HBM per device.

```python
import math
import jax
import jax.numpy as jnp
from jax import lax

COLS = 1024
ROWS_DEV = 512
NS = 8192
NBLK = 512
ROWS = 262144
SAMP_DEV = 16
CAP = 32
N_ROW = 64
N_GRP = 8


def draw_panel_rows(key, part):
    total_rows = ROWS_DEV * NBLK
    keys = jax.random.split(jax.random.fold_in(key, 11), 3)
    base_vals = jax.random.normal(keys[0], (total_rows, COLS), jnp.float32)
    row_scale = jnp.exp(jax.random.uniform(keys[1], (total_rows, 1), jnp.float32, math.log(0.5), math.log(5.0)))
    col_scale = jnp.exp(jax.random.uniform(keys[2], (1, COLS), jnp.float32, math.log(0.5), math.log(5.0)))
    return jnp.clip(base_vals * row_scale * col_scale, -300.0, 300.0).astype(jnp.bfloat16)


def draw_sample_rows(key, part):
    keys = jax.random.split(jax.random.fold_in(key, 23), 4)
    groups = NBLK // 4
    first_count = jax.random.randint(keys[0], (groups,), 0, 2 * SAMP_DEV + 1)
    second_count = jax.random.randint(keys[1], (groups,), 0, 2 * SAMP_DEV + 1 - first_count)
    third_count = 2 * SAMP_DEV - first_count - second_count
    counts = jnp.stack([jnp.full((groups,), CAP, jnp.int32), first_count, second_count, third_count], 1).reshape(NBLK)
    counts = counts[jax.random.permutation(keys[2], NBLK)]
    row_keys = jax.random.split(keys[3], NBLK)
    perms = jax.vmap(lambda row_key: jax.random.permutation(row_key, ROWS_DEV))(row_keys)
    ranks = jnp.argsort(perms, axis=1, stable=True).astype(jnp.int32)
    chosen = (ranks < counts[:, None]).reshape(-1)
    return jnp.nonzero(chosen, size=NS, fill_value=0)[0].astype(jnp.int32)


def with_ends(result, rng, smallest, high):
    dims = result.shape
    place = [jax.random.randint(jax.random.fold_in(rng, axis), (), 0, dims[axis]) for axis in range(len(dims))]
    result = result.at[tuple(place)].set(smallest)
    longest = dims.index(max(dims))
    place[longest] = (place[longest] + 1) % dims[longest]
    return result.at[tuple(place)].set(high)


def setup_inputs(seed: int = 0) -> dict:
    key_list = jax.random.split(jax.random.key(seed), 4)
    return {
        "panel_rows": draw_panel_rows(jax.random.fold_in(key_list[3], 71), 0),
        "sign_bits": with_ends(jax.random.randint(key_list[1], (ROWS,), 0, 2), jax.random.fold_in(key_list[1], 1), 0, 1).astype(jnp.int32),
        "sample_rows": draw_sample_rows(jax.random.fold_in(key_list[3], 71), 0),
    }


def hadamard(table_size):
    row_ids = lax.broadcasted_iota(jnp.int32, (table_size, table_size), 0)
    col_ids = lax.broadcasted_iota(jnp.int32, (table_size, table_size), 1)
    shared = row_ids & col_ids
    parity = jnp.zeros((table_size, table_size), jnp.int32)
    for bit_pos in range(table_size.bit_length() - 1):
        parity = parity ^ shared >> bit_pos & 1
    return (1 - 2 * parity).astype(jnp.float32)

def reference(panel_rows, sign_bits, sample_rows):
    flipped = panel_rows.astype(jnp.float32) * (1 - 2 * sign_bits).astype(jnp.float32)[:, None]
    blocks = flipped.reshape(N_ROW, N_GRP, ROWS_DEV, COLS)
    blocks = jnp.einsum('ar,rglc->aglc', hadamard(N_ROW), blocks, precision=lax.Precision.HIGHEST)
    blocks = jnp.einsum('bg,aglc->ablc', hadamard(N_GRP), blocks, precision=lax.Precision.HIGHEST)
    by_device = blocks.reshape(N_ROW * N_GRP, ROWS_DEV, COLS)
    local_table = hadamard(ROWS_DEV)
    norm_scale = 1.0 / math.sqrt(ROWS_DEV * N_ROW * N_GRP * NS)

    def one_block(sample_ids):
        device_ids = (sample_ids // ROWS_DEV).astype(jnp.int32)
        local_ids = (sample_ids % ROWS_DEV).astype(jnp.int32)
        table_rows = local_table[local_ids]
        source = by_device[device_ids]
        summed = jnp.einsum('sk,skc->sc', table_rows, source, precision=lax.Precision.HIGHEST)
        return (summed * norm_scale).astype(jnp.bfloat16)
    sketch = lax.map(one_block, sample_rows.reshape(-1, 64)).reshape(NS, COLS)
    gram_matrix = jnp.dot(sketch.T.astype(jnp.float32), sketch.astype(jnp.float32), preferred_element_type=jnp.float32)
    return jnp.linalg.cholesky(gram_matrix)
```

```python
import math

import jax
import jax.numpy as jnp
from jax import lax
from jax.experimental import pallas as pl
from jax.experimental.pallas import tpu as pltpu
from jax.sharding import PartitionSpec as P

HIGHEST = lax.Precision.HIGHEST
MESH = pl.DeviceIdType.MESH
BLOCK = 128
VMEM_LIMIT = 48 * 2**20


def hadamard(table_size, dtype):
    row_ids = lax.broadcasted_iota(jnp.int32, (table_size, table_size), 0)
    col_ids = lax.broadcasted_iota(jnp.int32, (table_size, table_size), 1)
    shared = row_ids & col_ids
    parity = jnp.zeros((table_size, table_size), jnp.int32)
    for bit_pos in range(table_size.bit_length() - 1):
        parity = parity ^ shared >> bit_pos & 1
    return (1 - 2 * parity).astype(dtype)


PARTS = ((0, 640, "xyz"), (640, 256, "yxz"), (896, 256, "zxy"))
SIZES = {"x": 4, "y": 8, "z": 8}


def place():
    row, grp = lax.axis_index("row"), lax.axis_index("grp")
    return {"core": row % 2, "x": row // 2 % 4, "z": row // 8, "y": grp}


def device(where, **other):
    at = dict(where, **other)
    return ((at["z"] * 4 + at["x"]) * 2 + at["core"], at["y"])


def sum_kernel(t_ref, o_ref, c_recv, acc, *rest):
    slots, (send_sem, recv_sem) = rest[:-2], rest[-2:]
    me = place()
    half = t_ref.shape[0] // 2
    barrier = pltpu.get_barrier_semaphore()
    peers = [device(me, core=1 - me["core"])]
    for axis, size in SIZES.items():
        peers += [device(me, **{axis: (me[axis] + off) % size}) for off in range(1, size)]
    for peer in peers:
        pl.semaphore_signal(barrier, inc=1, device_id=peer, device_id_type=MESH)
    pl.semaphore_wait(barrier, len(peers))

    def copy(src, dst, part, stage, off, peer):
        return pltpu.make_async_remote_copy(
            src_ref=src, dst_ref=dst, send_sem=send_sem.at[part, stage, off],
            recv_sem=recv_sem.at[part, stage, off], device_id=peer, device_id_type=MESH)

    def offset(value):
        return pl.multiple_of(value, 8)

    own = offset(me["core"] * half)
    other = offset((1 - me["core"]) * half)
    partner = device(me, core=1 - me["core"])
    flying = {}
    for part, (lo, width, _) in enumerate(PARTS):
        cols = pl.ds(lo, width)
        flying[part] = [copy(t_ref.at[pl.ds(other, half), cols], c_recv.at[:, cols], part, 0, 0, partner)]
        flying[part][0].start()
    started = list(flying.values())

    def peers_of(axis):
        size = SIZES[axis]
        return [(off, (me[axis] + off) % size) for off in range(1, size)]

    state = {}
    for part, (lo, width, order) in enumerate(PARTS):
        cols = pl.ds(lo, width)
        flying[part][0].wait()
        acc[:, cols] = t_ref[pl.ds(own, half), cols] + c_recv[:, cols]
        m = half // SIZES[order[0]]
        flying[part] = [
            copy(acc.at[pl.ds(offset(there * m), m), cols], slots[3 * part].at[off - 1], part, 1, off - 1,
                 device(me, **{order[0]: there}))
            for off, there in peers_of(order[0])]
        for c in flying[part]:
            c.start()
    for part, (lo, width, order) in enumerate(PARTS):
        cols = pl.ds(lo, width)
        m = half // SIZES[order[0]]
        m2 = m // SIZES[order[1]]
        base = offset(me[order[0]] * m)
        for c in flying[part]:
            c.wait()
        total = acc[pl.ds(base, m), cols]
        for k in range(SIZES[order[0]] - 1):
            total = total + slots[3 * part][k]
        acc[pl.ds(base, m), cols] = total
        flying[part] = [
            copy(acc.at[pl.ds(offset(base + there * m2), m2), cols], slots[3 * part + 1].at[off - 1], part, 2, off - 1,
                 device(me, **{order[1]: there}))
            for off, there in peers_of(order[1])]
        for c in flying[part]:
            c.start()
    for part, (lo, width, order) in enumerate(PARTS):
        cols = pl.ds(lo, width)
        m = half // SIZES[order[0]]
        m2 = m // SIZES[order[1]]
        base = offset(me[order[0]] * m + me[order[1]] * m2)
        for c in flying[part]:
            c.wait()
        total = acc[pl.ds(base, m2), cols]
        for k in range(SIZES[order[1]] - 1):
            total = total + slots[3 * part + 1][k]
        acc[pl.ds(base, m2), cols] = total
        flying[part] = [
            copy(acc.at[pl.ds(base, m2), cols], slots[3 * part + 2].at[off - 1], part, 3, off - 1,
                 device(me, **{order[2]: there}))
            for off, there in peers_of(order[2])]
        for c in flying[part]:
            c.start()
    for part, (lo, width, order) in enumerate(PARTS):
        cols = pl.ds(lo, width)
        m = half // SIZES[order[0]]
        m2 = m // SIZES[order[1]]
        base = offset(me[order[0]] * m + me[order[1]] * m2)
        for c in flying[part]:
            c.wait()
        total = acc[pl.ds(base, m2), cols]
        for k in range(SIZES[order[2]] - 1):
            total = total + slots[3 * part + 2][k]
        at = offset(own + base)
        o_ref[pl.ds(at, m2), cols] = total
        piece = o_ref.at[pl.ds(at, m2), cols]
        flying[part] = [
            copy(piece, piece, part, 4, off - 1, device(me, **{order[1]: there}))
            for off, there in peers_of(order[1])]
        for c in flying[part]:
            c.start()
    for part, (lo, width, order) in enumerate(PARTS):
        cols = pl.ds(lo, width)
        m = half // SIZES[order[0]]
        for c in flying[part]:
            c.wait()
        piece = o_ref.at[pl.ds(offset(own + me[order[0]] * m), m), cols]
        flying[part] = [
            copy(piece, piece, part, 5, off - 1, device(me, **{order[0]: there}))
            for off, there in peers_of(order[0])]
        for c in flying[part]:
            c.start()
    for part, (lo, width, order) in enumerate(PARTS):
        cols = pl.ds(lo, width)
        for c in flying[part]:
            c.wait()
        piece = o_ref.at[pl.ds(own, half), cols]
        flying[part] = [copy(piece, piece, part, 6, 0, partner)]
        flying[part][0].start()
    for part in range(len(PARTS)):
        flying[part][0].wait()


def sum_packed(packed):
    rows, width = packed.shape
    half = rows // 2
    slots = []
    for _, cols, order in PARTS:
        m = half // SIZES[order[0]]
        m2 = m // SIZES[order[1]]
        slots += [pltpu.VMEM((SIZES[order[0]] - 1, m, cols), jnp.float32),
                  pltpu.VMEM((SIZES[order[1]] - 1, m2, cols), jnp.float32),
                  pltpu.VMEM((SIZES[order[2]] - 1, m2, cols), jnp.float32)]
    return pl.pallas_call(
        sum_kernel,
        out_shape=jax.ShapeDtypeStruct(packed.shape, jnp.float32),
        in_specs=[pl.BlockSpec(memory_space=pltpu.VMEM)],
        out_specs=pl.BlockSpec(memory_space=pltpu.VMEM),
        scratch_shapes=[pltpu.VMEM((half, width), jnp.float32), pltpu.VMEM((half, width), jnp.float32), *slots,
                        pltpu.SemaphoreType.DMA((len(PARTS), 7, 7)), pltpu.SemaphoreType.DMA((len(PARTS), 7, 7))],
        compiler_params=pltpu.CompilerParams(collective_id=0, has_side_effects=True, vmem_limit_bytes=VMEM_LIMIT),
        name="gram_sum",
    )(packed)


def gram_kernel(w_ref, keep_ref, t_ref):
    size, n_cols = w_ref.shape
    table = hadamard(size, jnp.bfloat16)
    rest = w_ref[...]
    mixed = jnp.zeros_like(rest)
    for _ in range(3):
        head = rest.astype(jnp.bfloat16)
        mixed = mixed + jnp.dot(table, head, preferred_element_type=jnp.float32)
        rest = rest - head.astype(jnp.float32)
    sketch = (mixed * keep_ref[...]).astype(jnp.bfloat16)
    nb = n_cols // BLOCK
    dims = (((0,), (0,)), ((), ()))
    for j in range(nb):
        at = j * BLOCK
        prod = lax.dot_general(sketch[:, at:at + BLOCK], sketch[:, at:], dims, preferred_element_type=jnp.float32)
        fold = min(j, nb - 1 - j)
        start = 0 if j < nb // 2 else n_cols + BLOCK - (nb - j) * BLOCK
        t_ref[fold * BLOCK:(fold + 1) * BLOCK, start:start + (nb - j) * BLOCK] = prod


def partial_gram(w, keep):
    n_cols = w.shape[1]
    return pl.pallas_call(
        gram_kernel,
        out_shape=jax.ShapeDtypeStruct((n_cols // 2, n_cols + BLOCK), jnp.float32),
        in_specs=[pl.BlockSpec(memory_space=pltpu.VMEM)] * 2,
        out_specs=pl.BlockSpec(memory_space=pltpu.VMEM),
        compiler_params=pltpu.CompilerParams(vmem_limit_bytes=VMEM_LIMIT),
        name="gram_part",
    )(w, keep)


def lane(x, l):
    return jnp.broadcast_to(x[:, l:l + 1], (8, BLOCK))


def invert_factor(rows):
    groups = len(rows)
    lanes = lax.broadcasted_iota(jnp.int32, (8, BLOCK), 1)
    subs = lax.broadcasted_iota(jnp.int32, (8, BLOCK), 0)
    rows = list(rows)
    for b in range(groups):
        j0 = 8 * b
        here = rows[b]
        row = [jnp.broadcast_to(here[k:k + 1, :], (8, BLOCK)) for k in range(8)]
        s = {(k, l): lane(row[k], j0 + l) for k in range(8) for l in range(k, 8)}
        below = range(b + 1, groups)
        col = {(q, l): lane(rows[q], j0 + l) for q in below for l in range(8)}
        inside = (lanes >= j0) & (lanes < j0 + 8)
        row = [jnp.where(inside, (lanes == j0 + k).astype(jnp.float32), row[k]) for k in range(8)]
        mult = {}
        root = []
        for k in range(8):
            inv = 1.0 / s[k, k]
            root.append(lax.rsqrt(s[k, k]))
            for i in range(k + 1, 8):
                m = s[k, i] * inv
                for l in range(i, 8):
                    s[i, l] = s[i, l] - m * s[k, l]
                row[i] = row[i] - m * row[k]
            for q in below:
                m = col[q, k] * inv
                mult[q, k] = m
                for l in range(k + 1, 8):
                    col[q, l] = col[q, l] - m * s[k, l]
        for q in below:
            acc = jnp.where(inside, 0.0, rows[q])
            for k in range(8):
                acc = acc - mult[q, k] * row[k]
            rows[q] = acc
        out = row[0] * root[0]
        for k in range(1, 8):
            out = jnp.where(subs == k, row[k] * root[k], out)
        rows[b] = jnp.where(lanes <= subs + j0, out, 0.0)
    return rows


def cholesky_kernel(t_ref, o_ref, a):
    nb = a.shape[0] // BLOCK
    n_cols = nb * BLOCK
    me = place()
    my_row, my_grp = (me["z"] * 4 + me["x"]) * 2 + me["core"], me["y"]
    for j in range(nb):
        fold = min(j, nb - 1 - j)
        start = 0 if j < nb // 2 else n_cols + BLOCK - (nb - j) * BLOCK
        a[j * BLOCK:(j + 1) * BLOCK, j * BLOCK:] = t_ref[
            fold * BLOCK:(fold + 1) * BLOCK, start:start + (nb - j) * BLOCK]
    out_rows = o_ref.shape[0]
    o_ref[...] = jnp.zeros_like(o_ref)

    @pl.loop(0, nb)
    def _(j):
        base = pl.multiple_of(j * BLOCK, BLOCK)
        rows = [a[pl.ds(base + 8 * q, 8), pl.ds(base, BLOCK)] for q in range(BLOCK // 8)]
        inverse = jnp.concatenate(invert_factor(rows), axis=0)
        for t in range(nb):
            @pl.when(j == t)
            def _():
                lo = BLOCK * t
                upper = jnp.dot(inverse, a[lo:lo + BLOCK, lo:], precision=HIGHEST, preferred_element_type=jnp.float32)
                lower = upper.T
                a[lo:, lo:lo + BLOCK] = lower

                @pl.when((my_grp == t) & (my_row * out_rows >= lo))
                def _():
                    first = pl.multiple_of(my_row * out_rows, 8)
                    mine = a[pl.ds(first, out_rows), lo:lo + BLOCK]
                    r = lax.broadcasted_iota(jnp.int32, mine.shape, 0) + first
                    c = lax.broadcasted_iota(jnp.int32, mine.shape, 1) + lo
                    o_ref[...] = jnp.where(r >= c, mine, 0.0)

                for i in range(t + 1, nb):
                    at = BLOCK * i
                    a[at:at + BLOCK, at:] = a[at:at + BLOCK, at:] - jnp.dot(
                        lower[at - lo:at - lo + BLOCK], upper[:, at - lo:],
                        precision=HIGHEST, preferred_element_type=jnp.float32)


def cholesky_share(packed, n_cols, share):
    return pl.pallas_call(
        cholesky_kernel,
        out_shape=jax.ShapeDtypeStruct(share, jnp.float32),
        in_specs=[pl.BlockSpec(memory_space=pltpu.VMEM)],
        out_specs=pl.BlockSpec(memory_space=pltpu.VMEM),
        scratch_shapes=[pltpu.VMEM((n_cols, n_cols), jnp.float32)],
        compiler_params=pltpu.CompilerParams(vmem_limit_bytes=VMEM_LIMIT),
        name="cholesky",
    )(packed)


def local(panel_rows, sign_bits, sample_rows):
    rows_dev, n_cols = panel_rows.shape
    n_row = lax.axis_size("row")
    n_grp = lax.axis_size("grp")
    n_dev = n_row * n_grp
    flipped = panel_rows * (1 - 2 * sign_bits).astype(jnp.bfloat16)[:, None]
    local_mix = jnp.dot(hadamard(rows_dev, jnp.bfloat16), flipped, preferred_element_type=jnp.float32)
    mine = lax.all_to_all(local_mix, ("row", "grp"), 0, 0, tiled=True)
    norm_scale = 1.0 / math.sqrt(rows_dev * n_dev * sample_rows.shape[0])
    position = lax.axis_index("row") * n_grp + lax.axis_index("grp")
    ids = jnp.arange(n_dev, dtype=jnp.int32) * rows_dev + position
    sampled = jnp.any(sample_rows[None, :] == ids[:, None], axis=1)
    keep = jnp.where(sampled, norm_scale, 0.0).astype(jnp.float32)[:, None]
    packed = sum_packed(partial_gram(mine, keep))
    return cholesky_share(packed, n_cols, (n_cols // n_row, n_cols // n_grp))


def solution(mesh):
    return jax.shard_map(
        local,
        mesh=mesh,
        in_specs=(P(("row", "grp"), None), P(("row", "grp")), P()),
        out_specs=P("row", "grp"),
        check_vma=False,
    )
```

```python
import math

import jax
import jax.numpy as jnp
from jax import lax
from jax.experimental import pallas as pl
from jax.experimental.pallas import tpu as pltpu
from jax.sharding import PartitionSpec as P

HIGHEST = lax.Precision.HIGHEST
MESH = pl.DeviceIdType.MESH
BLOCK = 128
VMEM_LIMIT = 48 * 2**20


def hadamard(table_size, dtype):
    row_ids = lax.broadcasted_iota(jnp.int32, (table_size, table_size), 0)
    col_ids = lax.broadcasted_iota(jnp.int32, (table_size, table_size), 1)
    shared = row_ids & col_ids
    parity = jnp.zeros((table_size, table_size), jnp.int32)
    for bit_pos in range(table_size.bit_length() - 1):
        parity = parity ^ shared >> bit_pos & 1
    return (1 - 2 * parity).astype(dtype)


SIZES = {"x": 4, "y": 8, "z": 8}
STACKS = 4
N_BLOCKS = 8
UPPER = [(i, k) for i in range(N_BLOCKS) for k in range(i, N_BLOCKS)]
CHUNKS = ((4, "xyz"), (4, "xyz"), (8, "xyz"), (8, "yxz"), (12, "zxy"))
FIRST = [sum(n for n, _ in CHUNKS[:c]) for c in range(len(CHUNKS))]
BEFORE = ("g0 s0 g1 s1 g2 a0 a1 s2 g3 a0 a1 a2 g4 a0 a1 a2 s3 a0 a1 a2 a3 s4 a0 a1 a2 a3 a4 a0 a1 a2 a3 a4 f0")
BESIDE = ("f1 a2 a3 a4", "f2 a3 a4", "a3 a4", "f3 a4", "f4")


def staged(texts):
    reached = [0] * len(CHUNKS)
    out = []
    for text in texts:
        steps = []
        for word in text.split():
            c = int(word[1:])
            steps.append((word[0], c, reached[c]))
            reached[c] += word[0] == "a"
        out.append(steps)
    assert reached == [6] * len(CHUNKS)
    return out


def place():
    row, grp = lax.axis_index("row"), lax.axis_index("grp")
    return {"core": row % 2, "x": row // 2 % 4, "z": row // 8, "y": grp}


def device(where, **other):
    at = dict(where, **other)
    return ((at["z"] * 4 + at["x"]) * 2 + at["core"], at["y"])


def spot(block):
    index = UPPER.index(block)
    chunk = max(c for c in range(len(CHUNKS)) if FIRST[c] <= index)
    stack, col = divmod(index - FIRST[chunk], CHUNKS[chunk][0] // STACKS)
    return chunk, pl.ds(stack * BLOCK, BLOCK), pl.ds(col * BLOCK, BLOCK)


def offset(value):
    return pl.multiple_of(value, 8)


class Sum:
    def __init__(self, chunk, refs, send_sem, recv_sem, me):
        order = CHUNKS[chunk][1]
        self.part, self.near, self.slots, self.full = refs[0], refs[1], refs[2:5], refs[5]
        self.order, self.chunk, self.send_sem, self.recv_sem, self.me = order, chunk, send_sem, recv_sem, me
        self.half = self.part.shape[0] // 2
        self.own = offset(me["core"] * self.half)
        self.m1 = self.half // SIZES[order[0]]
        self.m2 = self.m1 // SIZES[order[1]]
        self.base1 = offset(self.own + me[order[0]] * self.m1)
        self.base2 = offset(self.base1 + me[order[1]] * self.m2)

    def copy(self, src, dst, stage, k, peer):
        return pltpu.make_async_remote_copy(
            src_ref=src, dst_ref=dst, send_sem=self.send_sem.at[self.chunk, stage, k],
            recv_sem=self.recv_sem.at[self.chunk, stage, k], device_id=peer, device_id_type=MESH)

    def peers(self, axis):
        size = SIZES[axis]
        there = [(self.me[axis] + off) % size for off in range(1, size)]
        return [(k, t, device(self.me, **{axis: t})) for k, t in enumerate(there)]

    def copies(self, stage):
        part, full, order = self.part, self.full, self.order
        if stage in (0, 6):
            partner = device(self.me, core=1 - self.me["core"])
            if stage == 0:
                other = offset((1 - self.me["core"]) * self.half)
                return [self.copy(part.at[pl.ds(other, self.half)], self.near, stage, 0, partner)]
            piece = full.at[pl.ds(self.own, self.half)]
            return [self.copy(piece, piece, stage, 0, partner)]
        axis = order[{1: 0, 2: 1, 3: 2, 4: 1, 5: 0}[stage]]
        out = []
        for k, t, peer in self.peers(axis):
            if stage == 1:
                src, dst = part.at[pl.ds(offset(self.own + t * self.m1), self.m1)], self.slots[0].at[k]
            elif stage == 2:
                src, dst = part.at[pl.ds(offset(self.base1 + t * self.m2), self.m2)], self.slots[1].at[k]
            elif stage == 3:
                src, dst = part.at[pl.ds(self.base2, self.m2)], self.slots[2].at[k]
            else:
                at, m = (self.base2, self.m2) if stage == 4 else (self.base1, self.m1)
                src = dst = full.at[pl.ds(at, m)]
            out.append(self.copy(src, dst, stage, k, peer))
        return out

    def start(self, stage):
        for c in self.copies(stage):
            c.start()

    def finish(self, stage):
        for c in self.copies(stage):
            c.wait()

    def advance(self, stage):
        self.finish(stage)
        part = self.part
        if stage == 0:
            part[pl.ds(self.own, self.half)] = part[pl.ds(self.own, self.half)] + self.near[...]
        elif stage < 4:
            at, m = (self.base1, self.m1) if stage == 1 else (self.base2, self.m2)
            total = part[pl.ds(at, m)]
            slots = self.slots[stage - 1]
            for k in range(slots.shape[0]):
                total = total + slots[k]
            into = self.full if stage == 3 else part
            into[pl.ds(at, m)] = total
        self.start(stage + 1)


def buffers(blocks, order):
    rows, cols = STACKS * BLOCK, blocks // STACKS * BLOCK
    half = rows // 2
    m1 = half // SIZES[order[0]]
    m2 = m1 // SIZES[order[1]]
    shapes = [(rows, cols), (half, cols), (SIZES[order[0]] - 1, m1, cols), (SIZES[order[1]] - 1, m2, cols),
              (SIZES[order[2]] - 1, m2, cols), (rows, cols)]
    return [pltpu.VMEM(shape, jnp.float32) for shape in shapes]


def lane(x, l):
    return jnp.broadcast_to(x[:, l:l + 1], (8, BLOCK))


def invert_factor(rows, midway):
    groups = len(rows)
    lanes = lax.broadcasted_iota(jnp.int32, (8, BLOCK), 1)
    subs = lax.broadcasted_iota(jnp.int32, (8, BLOCK), 0)
    rows = list(rows)
    for b in range(groups):
        if b == groups // 2:
            midway()
        j0 = 8 * b
        here = rows[b]
        row = [jnp.broadcast_to(here[k:k + 1, :], (8, BLOCK)) for k in range(8)]
        s = {(k, l): lane(row[k], j0 + l) for k in range(8) for l in range(k, 8)}
        below = range(b + 1, groups)
        col = {(q, l): lane(rows[q], j0 + l) for q in below for l in range(8)}
        inside = (lanes >= j0) & (lanes < j0 + 8)
        row = [jnp.where(inside, (lanes == j0 + k).astype(jnp.float32), row[k]) for k in range(8)]
        mult = {}
        root = []
        for k in range(8):
            inv = 1.0 / s[k, k]
            root.append(lax.rsqrt(s[k, k]))
            for i in range(k + 1, 8):
                m = s[k, i] * inv
                for l in range(i, 8):
                    s[i, l] = s[i, l] - m * s[k, l]
                row[i] = row[i] - m * row[k]
            for q in below:
                m = col[q, k] * inv
                mult[q, k] = m
                for l in range(k + 1, 8):
                    col[q, l] = col[q, l] - m * s[k, l]
        for q in below:
            acc = jnp.where(inside, 0.0, rows[q])
            for k in range(8):
                acc = acc - mult[q, k] * row[k]
            rows[q] = acc
        out = row[0] * root[0]
        for k in range(1, 8):
            out = jnp.where(subs == k, row[k] * root[k], out)
        rows[b] = jnp.where(lanes <= subs + j0, out, 0.0)
    return rows


def factor_kernel(w_ref, keep_ref, o_ref, sketch, a, send_sem, recv_sem, *chunk_refs):
    me = place()
    barrier = pltpu.get_barrier_semaphore()
    peers = [device(me, core=1 - me["core"])]
    for axis, size in SIZES.items():
        peers += [device(me, **{axis: (me[axis] + off) % size}) for off in range(1, size)]
    for peer in peers:
        pl.semaphore_signal(barrier, inc=1, device_id=peer, device_id_type=MESH)

    size = w_ref.shape[0]
    table = hadamard(size, jnp.bfloat16)
    rest = w_ref[...]
    mixed = jnp.zeros_like(rest)
    for _ in range(3):
        head = rest.astype(jnp.bfloat16)
        mixed = mixed + jnp.dot(table, head, preferred_element_type=jnp.float32)
        rest = rest - head.astype(jnp.float32)
    sketch[...] = (mixed * keep_ref[...]).astype(jnp.bfloat16)

    per = len(chunk_refs) // len(CHUNKS)
    sums = [Sum(c, chunk_refs[per * c:per * c + per], send_sem, recv_sem, me) for c in range(len(CHUNKS))]

    def gram(c):
        blocks = UPPER[FIRST[c]:FIRST[c] + CHUNKS[c][0]]
        for i in sorted({i for i, _ in blocks}):
            ks = [k for bi, k in blocks if bi == i]
            wide = lax.dot_general(
                sketch[:, i * BLOCK:(i + 1) * BLOCK], sketch[:, ks[0] * BLOCK:(ks[-1] + 1) * BLOCK],
                (((0,), (0,)), ((), ())), preferred_element_type=jnp.float32)
            for n, k in enumerate(ks):
                _, rows, cols = spot((i, k))
                sums[c].part[rows, cols] = wide[:, n * BLOCK:(n + 1) * BLOCK]

    def run(steps):
        for what, c, stage in steps:
            if what == "g":
                gram(c)
                if c == 0:
                    pl.semaphore_wait(barrier, len(peers))
            elif what == "s":
                sums[c].start(stage)
            elif what == "a":
                sums[c].advance(stage)
            else:
                sums[c].finish(stage)

    before, *beside = staged((BEFORE, *BESIDE))
    run(before)

    my_row, my_grp = (me["z"] * SIZES["x"] + me["x"]) * 2 + me["core"], me["y"]
    out_rows = o_ref.shape[0]
    o_ref[...] = jnp.zeros_like(o_ref)

    def place_block(i, k):
        chunk, rows, cols = spot((i, k))
        a[i * BLOCK:(i + 1) * BLOCK, k * BLOCK:(k + 1) * BLOCK] = sums[chunk].full[rows, cols]

    def updated(t, first):
        lo, col = BLOCK * t, BLOCK * first
        a[lo:lo + BLOCK, col:] = a[lo:lo + BLOCK, col:] - jnp.dot(
            a[lo:lo + BLOCK, :lo], a[:lo, col:], precision=HIGHEST, preferred_element_type=jnp.float32)

    place_block(0, 0)

    @pl.loop(0, N_BLOCKS)
    def _(j):
        for t in range(1, N_BLOCKS):
            @pl.when(j == t)
            def _():
                for k in range(t, N_BLOCKS):
                    place_block(t, k)
                updated(t, t)

        base = pl.multiple_of(j * BLOCK, BLOCK)
        rows = [a[pl.ds(base + 8 * q, 8), pl.ds(base, BLOCK)] for q in range(BLOCK // 8)]

        def midway():
            for t, steps in enumerate(beside[0::2]):
                @pl.when(j == t)
                def _():
                    run(steps)

        inverse = jnp.concatenate(invert_factor(rows, midway), axis=0)
        for t in range(N_BLOCKS):
            @pl.when(j == t)
            def _():
                lo = BLOCK * t
                if t == 0:
                    for k in range(1, N_BLOCKS):
                        place_block(0, k)
                upper = jnp.dot(inverse, a[lo:lo + BLOCK, lo:], precision=HIGHEST, preferred_element_type=jnp.float32)
                a[lo:lo + BLOCK, lo:] = upper
                a[lo:, lo:lo + BLOCK] = upper.T

                @pl.when((my_grp == t) & (my_row * out_rows >= lo))
                def _():
                    first = offset(my_row * out_rows)
                    mine = a[pl.ds(first, out_rows), lo:lo + BLOCK]
                    r = lax.broadcasted_iota(jnp.int32, mine.shape, 0) + first
                    c = lax.broadcasted_iota(jnp.int32, mine.shape, 1) + lo
                    o_ref[...] = jnp.where(r >= c, mine, 0.0)

                if 2 * t + 1 < len(beside):
                    run(beside[2 * t + 1])


def factor_share(w, keep, share):
    n_cols = w.shape[1]
    scratch = [pltpu.VMEM(w.shape, jnp.bfloat16), pltpu.VMEM((n_cols, n_cols), jnp.float32)]
    scratch += [pltpu.SemaphoreType.DMA((len(CHUNKS), 7, 7))] * 2
    for blocks, order in CHUNKS:
        scratch += buffers(blocks, order)
    return pl.pallas_call(
        factor_kernel,
        out_shape=jax.ShapeDtypeStruct(share, jnp.float32),
        in_specs=[pl.BlockSpec(memory_space=pltpu.VMEM)] * 2,
        out_specs=pl.BlockSpec(memory_space=pltpu.VMEM),
        scratch_shapes=scratch,
        compiler_params=pltpu.CompilerParams(collective_id=0, has_side_effects=True, vmem_limit_bytes=VMEM_LIMIT),
        name="factor",
    )(w, keep)


def local(panel_rows, sign_bits, sample_rows):
    rows_dev, n_cols = panel_rows.shape
    n_row = lax.axis_size("row")
    n_grp = lax.axis_size("grp")
    n_dev = n_row * n_grp
    flipped = panel_rows * (1 - 2 * sign_bits).astype(jnp.bfloat16)[:, None]
    local_mix = jnp.dot(hadamard(rows_dev, jnp.bfloat16), flipped, preferred_element_type=jnp.float32)
    mine = lax.all_to_all(local_mix, ("row", "grp"), 0, 0, tiled=True)
    norm_scale = 1.0 / math.sqrt(rows_dev * n_dev * sample_rows.shape[0])
    position = lax.axis_index("row") * n_grp + lax.axis_index("grp")
    ids = jnp.arange(n_dev, dtype=jnp.int32) * rows_dev + position
    sampled = jnp.any(sample_rows[None, :] == ids[:, None], axis=1)
    keep = jnp.where(sampled, norm_scale, 0.0).astype(jnp.float32)[:, None]
    return factor_share(mine, keep, (n_cols // n_row, n_cols // n_grp))


def solution(mesh):
    return jax.shard_map(
        local,
        mesh=mesh,
        in_specs=(P(("row", "grp"), None), P(("row", "grp")), P()),
        out_specs=P("row", "grp"),
        check_vma=False,
    )
```

```python
import math

import jax
import jax.numpy as jnp
from jax import lax
from jax.experimental import pallas as pl
from jax.experimental.pallas import tpu as pltpu
from jax.sharding import PartitionSpec as P

HIGHEST = lax.Precision.HIGHEST
MESH = pl.DeviceIdType.MESH
BLOCK = 128
VMEM_LIMIT = 48 * 2**20


def hadamard(table_size, dtype):
    row_ids = lax.broadcasted_iota(jnp.int32, (table_size, table_size), 0)
    col_ids = lax.broadcasted_iota(jnp.int32, (table_size, table_size), 1)
    shared = row_ids & col_ids
    parity = jnp.zeros((table_size, table_size), jnp.int32)
    for bit_pos in range(table_size.bit_length() - 1):
        parity = parity ^ shared >> bit_pos & 1
    return (1 - 2 * parity).astype(dtype)


SIZES = {"x": 4, "y": 8, "z": 8}
STACKS = 4
N_BLOCKS = 8
UPPER = [(i, k) for i in range(N_BLOCKS) for k in range(i, N_BLOCKS)]
CHUNKS = ((20, "xyz"), (8, "yxz"), (8, "zxy"))
FIRST = [sum(n for n, _ in CHUNKS[:c]) for c in range(len(CHUNKS))]
BEFORE = ("g0", "s0", "g1", "s1", "g2", "s2", "a0", "a1", "a2", "a0", "a1", "a2", "a0", "a1", "a2", "a0", "a1", "a2", "a0", "a1", "a2", "a0", "a1", "a2", "f0", "f1", "f2")
BESIDE = ()


def staged(texts):
    reached = [0] * len(CHUNKS)
    out = []
    for text in texts:
        steps = []
        for word in text:
            c = int(word[1:])
            steps.append((word[0], c, reached[c]))
            reached[c] += word[0] == "a"
        out.append(steps)
    assert reached == [6] * len(CHUNKS)
    return out


def place():
    row, grp = lax.axis_index("row"), lax.axis_index("grp")
    return {"core": row % 2, "x": row // 2 % 4, "z": row // 8, "y": grp}


def device(where, **other):
    at = dict(where, **other)
    return ((at["z"] * 4 + at["x"]) * 2 + at["core"], at["y"])


def spot(block):
    index = UPPER.index(block)
    chunk = max(c for c in range(len(CHUNKS)) if FIRST[c] <= index)
    stack, col = divmod(index - FIRST[chunk], CHUNKS[chunk][0] // STACKS)
    return chunk, pl.ds(stack * BLOCK, BLOCK), pl.ds(col * BLOCK, BLOCK)


def offset(value):
    return pl.multiple_of(value, 8)


class Sum:
    def __init__(self, chunk, refs, send_sem, recv_sem, me):
        order = CHUNKS[chunk][1]
        self.part, self.near, self.slots, self.full = refs[0], refs[1], refs[2:5], refs[5]
        self.order, self.chunk, self.send_sem, self.recv_sem, self.me = order, chunk, send_sem, recv_sem, me
        self.half = self.part.shape[0] // 2
        self.own = offset(me["core"] * self.half)
        self.m1 = self.half // SIZES[order[0]]
        self.m2 = self.m1 // SIZES[order[1]]
        self.base1 = offset(self.own + me[order[0]] * self.m1)
        self.base2 = offset(self.base1 + me[order[1]] * self.m2)

    def copy(self, src, dst, stage, k, peer):
        return pltpu.make_async_remote_copy(
            src_ref=src, dst_ref=dst, send_sem=self.send_sem.at[self.chunk, stage, k],
            recv_sem=self.recv_sem.at[self.chunk, stage, k], device_id=peer, device_id_type=MESH)

    def peers(self, axis):
        size = SIZES[axis]
        there = [(self.me[axis] + off) % size for off in range(1, size)]
        return [(k, t, device(self.me, **{axis: t})) for k, t in enumerate(there)]

    def copies(self, stage):
        part, full, order = self.part, self.full, self.order
        if stage in (0, 6):
            partner = device(self.me, core=1 - self.me["core"])
            if stage == 0:
                other = offset((1 - self.me["core"]) * self.half)
                return [self.copy(part.at[pl.ds(other, self.half)], self.near, stage, 0, partner)]
            piece = full.at[pl.ds(self.own, self.half)]
            return [self.copy(piece, piece, stage, 0, partner)]
        axis = order[{1: 0, 2: 1, 3: 2, 4: 1, 5: 0}[stage]]
        out = []
        for k, t, peer in self.peers(axis):
            if stage == 1:
                src, dst = part.at[pl.ds(offset(self.own + t * self.m1), self.m1)], self.slots[0].at[k]
            elif stage == 2:
                src, dst = part.at[pl.ds(offset(self.base1 + t * self.m2), self.m2)], self.slots[1].at[k]
            elif stage == 3:
                src, dst = part.at[pl.ds(self.base2, self.m2)], self.slots[2].at[k]
            else:
                at, m = (self.base2, self.m2) if stage == 4 else (self.base1, self.m1)
                src = dst = full.at[pl.ds(at, m)]
            out.append(self.copy(src, dst, stage, k, peer))
        return out

    def start(self, stage):
        for c in self.copies(stage):
            c.start()

    def finish(self, stage):
        for c in self.copies(stage):
            c.wait()

    def advance(self, stage):
        self.finish(stage)
        part = self.part
        if stage == 0:
            part[pl.ds(self.own, self.half)] = part[pl.ds(self.own, self.half)] + self.near[...]
        elif stage < 4:
            at, m = (self.base1, self.m1) if stage == 1 else (self.base2, self.m2)
            total = part[pl.ds(at, m)]
            slots = self.slots[stage - 1]
            for k in range(slots.shape[0]):
                total = total + slots[k]
            into = self.full if stage == 3 else part
            into[pl.ds(at, m)] = total
        self.start(stage + 1)


def buffers(blocks, order):
    rows, cols = STACKS * BLOCK, blocks // STACKS * BLOCK
    half = rows // 2
    m1 = half // SIZES[order[0]]
    m2 = m1 // SIZES[order[1]]
    shapes = [(rows, cols), (half, cols), (SIZES[order[0]] - 1, m1, cols), (SIZES[order[1]] - 1, m2, cols),
              (SIZES[order[2]] - 1, m2, cols), (rows, cols)]
    return [pltpu.VMEM(shape, jnp.float32) for shape in shapes]


def hadamard_list(size):
    return [[1 - 2 * ((i & k).bit_count() % 2) for k in range(size)] for i in range(size)]


def lane(x, l):
    return jnp.broadcast_to(x[:, l:l + 1], (8, BLOCK))


def invert_factor(rows, midway):
    groups = len(rows)
    lanes = lax.broadcasted_iota(jnp.int32, (8, BLOCK), 1)
    subs = lax.broadcasted_iota(jnp.int32, (8, BLOCK), 0)
    rows = list(rows)
    for b in range(groups):
        if b == groups // 2:
            midway()
        j0 = 8 * b
        here = rows[b]
        row = [jnp.broadcast_to(here[k:k + 1, :], (8, BLOCK)) for k in range(8)]
        s = {(k, l): lane(row[k], j0 + l) for k in range(8) for l in range(k, 8)}
        below = range(b + 1, groups)
        col = {(q, l): lane(rows[q], j0 + l) for q in below for l in range(8)}
        inside = (lanes >= j0) & (lanes < j0 + 8)
        row = [jnp.where(inside, (lanes == j0 + k).astype(jnp.float32), row[k]) for k in range(8)]
        mult = {}
        root = []
        for k in range(8):
            inv = 1.0 / s[k, k]
            root.append(lax.rsqrt(s[k, k]))
            for i in range(k + 1, 8):
                m = s[k, i] * inv
                for l in range(i, 8):
                    s[i, l] = s[i, l] - m * s[k, l]
                row[i] = row[i] - m * row[k]
            for q in below:
                m = col[q, k] * inv
                mult[q, k] = m
                for l in range(k + 1, 8):
                    col[q, l] = col[q, l] - m * s[k, l]
        for q in below:
            acc = jnp.where(inside, 0.0, rows[q])
            for k in range(8):
                acc = acc - mult[q, k] * row[k]
            rows[q] = acc
        out = row[0] * root[0]
        for k in range(1, 8):
            out = jnp.where(subs == k, row[k] * root[k], out)
        rows[b] = jnp.where(lanes <= subs + j0, out, 0.0)
    return rows


def factor_kernel(panel_ref, sign_ref, ids_ref, o_ref, table, mixed, mid_y, mid_r, got, keep, sketch, a,
                  swap_sem, send_sem, recv_sem, *chunk_refs):
    me = place()
    n_dev = got.shape[0] * got.shape[1]
    rows_dev, n_cols = panel_ref.shape
    n_row, n_grp, n_chip = got.shape[0], got.shape[1], got.shape[0] // 2
    my_row, my_grp, core = (me["z"] * SIZES["x"] + me["x"]) * 2 + me["core"], me["y"], me["core"]
    my_chip = my_row // 2
    half = rows_dev // 2

    barrier = pltpu.get_barrier_semaphore()

    def next_chip(off):
        return (my_chip + off) % n_chip

    def greet(row, grp):
        pl.semaphore_signal(barrier, inc=1, device_id=(row, grp), device_id_type=MESH)

    for off in range(1, n_grp):
        greet(my_row, (my_grp + off) % n_grp)
    greet(my_row + 1 - 2 * core, my_grp)

    @pl.loop(1, n_chip)
    def _(off):
        greet(2 * next_chip(off), my_grp)
        greet(2 * next_chip(off) + 1, my_grp)

    base = hadamard(BLOCK, jnp.float32)
    corner = hadamard_list(rows_dev // BLOCK)
    flip = (1 - 2 * sign_ref[...]).astype(jnp.float32)
    for i, signs in enumerate(corner):
        for k, sign in enumerate(signs):
            table[i * BLOCK:(i + 1) * BLOCK, k * BLOCK:(k + 1) * BLOCK] = (base * sign).astype(jnp.bfloat16)
    flat = mixed.reshape(rows_dev * 8, BLOCK)

    def mix(h):
        signed = (table[h * half:(h + 1) * half, :].astype(jnp.float32) * flip).astype(jnp.bfloat16)
        part = jnp.dot(signed, panel_ref[...], preferred_element_type=jnp.float32)
        for k in range(8):
            flat[pl.ds(h * half * 8 + k, half, 8), :] = part[:, k * BLOCK:(k + 1) * BLOCK]

    def remote(src, dst, sem, row, grp):
        return pltpu.make_async_remote_copy(
            src_ref=src, dst_ref=dst, send_sem=swap_sem.at[0, sem], recv_sem=swap_sem.at[1, sem],
            device_id=(row, grp), device_id_type=MESH)

    def here(src, dst, sem):
        return pltpu.make_async_copy(src, dst, swap_sem.at[0, sem])

    def waits(sent, received, sem):
        if sent is not None:
            remote(sent, sent, sem, my_row, my_grp).wait_send()
        if received is not None:
            remote(received, received, sem, my_row, my_grp).wait_recv()

    mix(0)
    pl.semaphore_wait(barrier, n_row + n_grp - 2)
    per_grp = half // n_grp
    for off in range(1, n_grp):
        t = (my_grp + off) % n_grp
        remote(mixed.at[pl.ds(t * per_grp, per_grp)], mid_y.at[my_grp], off, my_row, t).start()
    own_y = here(mixed.at[pl.ds(my_grp * per_grp, per_grp)], mid_y.at[my_grp], 8)
    own_y.start()
    mix(1)

    def to_second(chip):
        return remote(mixed.at[pl.ds(half + chip * n_grp, n_grp)], mid_r.at[my_row], 0, 2 * chip + 1, my_grp)

    own_r = here(mixed.at[pl.ds(half + my_chip * n_grp, n_grp)], mid_r.at[my_row], 9)

    @pl.loop(1, n_chip)
    def _(off):
        to_second(next_chip(off)).start()

    @pl.when(core == 0)
    def _():
        to_second(my_chip).start()

    @pl.when(core == 1)
    def _():
        own_r.start()

    position = jnp.where(core == 0, my_grp * n_chip + my_chip, half + my_chip * n_grp + my_grp)
    wanted = lax.broadcasted_iota(jnp.int32, (n_dev, BLOCK), 0) * rows_dev + position
    hits = jnp.zeros((n_dev, BLOCK), jnp.int32)
    for i in range(ids_ref.shape[0]):
        hits = jnp.where(ids_ref[i:i + 1, :] == wanted, 1, hits)
    norm_scale = 1.0 / math.sqrt(rows_dev * n_dev * ids_ref.shape[0] * ids_ref.shape[1])
    keep[...] = jnp.max(hits, axis=1, keepdims=True).astype(jnp.float32) * norm_scale

    for off in range(1, n_grp):
        remote(mid_y.at[0], mid_y.at[0], off, my_row, my_grp).wait()
    own_y.wait()

    def to_first(chip):
        return remote(mid_y.at[:, chip], got.at[my_row], 10, 2 * chip, my_grp)

    own_f = here(mid_y.at[:, my_chip], got.at[my_row], 11)

    @pl.loop(1, n_chip)
    def _(off):
        to_first(next_chip(off)).start()

    @pl.when(core == 1)
    def _():
        to_first(my_chip).start()
        own_r.wait()
        waits(mid_r.at[pl.ds(0, n_chip - 1)], mid_r.at[pl.ds(0, n_row - 1)], 0)
        for off in range(1, n_grp):
            t = (my_grp + off) % n_grp
            remote(mid_r.at[:, t], got.at[:, my_grp], 11 + off, my_row, t).start()
        own_g = here(mid_r.at[:, my_grp], got.at[:, my_grp], 11)
        own_g.start()
        waits(got.at[pl.ds(0, n_chip)], None, 10)
        for off in range(1, n_grp):
            remote(got.at[:, 0], got.at[:, 0], 11 + off, my_row, my_grp).wait()
        own_g.wait()

    @pl.when(core == 0)
    def _():
        own_f.start()
        waits(mid_r.at[pl.ds(0, n_chip)], None, 0)
        waits(got.at[pl.ds(0, n_chip - 1)], got.at[pl.ds(0, n_row - 1)], 10)
        own_f.wait()

    flat_got = got.reshape(n_dev * 8, BLOCK)
    for k in range(0, 8, 2):
        rest = jnp.concatenate([flat_got[pl.ds(k, n_dev, 8), :], flat_got[pl.ds(k + 1, n_dev, 8), :]], axis=1)
        total = jnp.zeros_like(rest)
        for _ in range(3):
            top = rest.astype(jnp.bfloat16)
            total = total + jnp.dot(table[...], top, preferred_element_type=jnp.float32)
            rest = rest - top.astype(jnp.float32)
        sketch[:, k * BLOCK:(k + 2) * BLOCK] = (total * keep[...]).astype(jnp.bfloat16)

    per = len(chunk_refs) // len(CHUNKS)
    sums = [Sum(c, chunk_refs[per * c:per * c + per], send_sem, recv_sem, me) for c in range(len(CHUNKS))]

    def gram(c):
        blocks = UPPER[FIRST[c]:FIRST[c] + CHUNKS[c][0]]
        for i in sorted({i for i, _ in blocks}):
            ks = [k for bi, k in blocks if bi == i]
            wide = lax.dot_general(
                sketch[:, i * BLOCK:(i + 1) * BLOCK], sketch[:, ks[0] * BLOCK:(ks[-1] + 1) * BLOCK],
                (((0,), (0,)), ((), ())), preferred_element_type=jnp.float32)
            for n, k in enumerate(ks):
                _, rows, cols = spot((i, k))
                sums[c].part[rows, cols] = wide[:, n * BLOCK:(n + 1) * BLOCK]

    def run(steps):
        for what, c, stage in steps:
            if what == "g":
                gram(c)
            elif what == "s":
                sums[c].start(stage)
            elif what == "a":
                sums[c].advance(stage)
            else:
                sums[c].finish(stage)

    before, *beside = staged((BEFORE, *BESIDE))
    run(before)

    out_rows = o_ref.shape[0]
    o_ref[...] = jnp.zeros_like(o_ref)

    def place_block(i, k):
        chunk, rows, cols = spot((i, k))
        a[i * BLOCK:(i + 1) * BLOCK, k * BLOCK:(k + 1) * BLOCK] = sums[chunk].full[rows, cols]

    def updated(t, first):
        lo, col = BLOCK * t, BLOCK * first
        a[lo:lo + BLOCK, col:] = a[lo:lo + BLOCK, col:] - jnp.dot(
            a[lo:lo + BLOCK, :lo], a[:lo, col:], precision=HIGHEST, preferred_element_type=jnp.float32)

    place_block(0, 0)

    @pl.loop(0, N_BLOCKS)
    def _(j):
        for t in range(1, N_BLOCKS):
            @pl.when(j == t)
            def _():
                for k in range(t, N_BLOCKS):
                    place_block(t, k)
                updated(t, t)

        base = pl.multiple_of(j * BLOCK, BLOCK)
        rows = [a[pl.ds(base + 8 * q, 8), pl.ds(base, BLOCK)] for q in range(BLOCK // 8)]

        def midway():
            for t, steps in enumerate(beside[0::2]):
                @pl.when(j == t)
                def _():
                    run(steps)

        inverse = jnp.concatenate(invert_factor(rows, midway), axis=0)
        for t in range(N_BLOCKS):
            @pl.when(j == t)
            def _():
                lo = BLOCK * t
                if t == 0:
                    for k in range(1, N_BLOCKS):
                        place_block(0, k)
                upper = jnp.dot(inverse, a[lo:lo + BLOCK, lo:], precision=HIGHEST, preferred_element_type=jnp.float32)
                a[lo:lo + BLOCK, lo:] = upper
                a[lo:, lo:lo + BLOCK] = upper.T

                @pl.when((my_grp == t) & (my_row * out_rows >= lo))
                def _():
                    first = offset(my_row * out_rows)
                    mine = a[pl.ds(first, out_rows), lo:lo + BLOCK]
                    r = lax.broadcasted_iota(jnp.int32, mine.shape, 0) + first
                    c = lax.broadcasted_iota(jnp.int32, mine.shape, 1) + lo
                    o_ref[...] = jnp.where(r >= c, mine, 0.0)

                if 2 * t + 1 < len(beside):
                    run(beside[2 * t + 1])


def factor_share(panel_rows, signs, ids, n_row, n_grp):
    rows_dev, n_cols = panel_rows.shape
    tile = (n_cols // BLOCK, BLOCK)
    scratch = [
        pltpu.VMEM((rows_dev, rows_dev), jnp.bfloat16),
        pltpu.VMEM((rows_dev, *tile), jnp.float32),
        pltpu.VMEM((n_grp, n_row // 2, *tile), jnp.float32),
        pltpu.VMEM((n_row, n_grp, *tile), jnp.float32),
        pltpu.VMEM((n_row, n_grp, *tile), jnp.float32),
        pltpu.VMEM((n_row * n_grp, 1), jnp.float32),
        pltpu.VMEM((n_row * n_grp, n_cols), jnp.bfloat16),
        pltpu.VMEM((n_cols, n_cols), jnp.float32),
        pltpu.SemaphoreType.DMA((2, 19)),
    ]
    scratch += [pltpu.SemaphoreType.DMA((len(CHUNKS), 7, 7))] * 2
    for blocks, order in CHUNKS:
        scratch += buffers(blocks, order)
    return pl.pallas_call(
        factor_kernel,
        out_shape=jax.ShapeDtypeStruct((n_cols // n_row, n_cols // n_grp), jnp.float32),
        in_specs=[pl.BlockSpec(memory_space=pltpu.VMEM)] * 3,
        out_specs=pl.BlockSpec(memory_space=pltpu.VMEM),
        scratch_shapes=scratch,
        compiler_params=pltpu.CompilerParams(collective_id=0, has_side_effects=True, vmem_limit_bytes=VMEM_LIMIT),
        name="factor",
    )(panel_rows, signs, ids)


def local(panel_rows, sign_bits, sample_rows):
    return factor_share(panel_rows, sign_bits[None, :], sample_rows.reshape(-1, BLOCK),
                        lax.axis_size("row"), lax.axis_size("grp"))


def solution(mesh):
    return jax.shard_map(
        local,
        mesh=mesh,
        in_specs=(P(("row", "grp"), None), P(("row", "grp")), P()),
        out_specs=P("row", "grp"),
        check_vma=False,
    )
```

```python
import math

import jax
import jax.numpy as jnp
from jax import lax
from jax.experimental import pallas as pl
from jax.experimental.pallas import tpu as pltpu
from jax.sharding import PartitionSpec as P

HIGHEST = lax.Precision.HIGHEST
MESH = pl.DeviceIdType.MESH
BLOCK = 128
VMEM_LIMIT = 48 * 2**20


def hadamard(table_size, dtype):
    row_ids = lax.broadcasted_iota(jnp.int32, (table_size, table_size), 0)
    col_ids = lax.broadcasted_iota(jnp.int32, (table_size, table_size), 1)
    shared = row_ids & col_ids
    parity = jnp.zeros((table_size, table_size), jnp.int32)
    for bit_pos in range(table_size.bit_length() - 1):
        parity = parity ^ shared >> bit_pos & 1
    return (1 - 2 * parity).astype(dtype)


SIZES = {"x": 4, "y": 8, "z": 8}
STACKS = 4
N_BLOCKS = 8
UPPER = [(i, k) for i in range(N_BLOCKS) for k in range(i, N_BLOCKS)]
CHUNKS = ((12, "xyz"), (8, "xzy"), (8, "yxz"), (8, "zxy"))
FIRST = [sum(n for n, _ in CHUNKS[:c]) for c in range(len(CHUNKS))]
BEFORE = ("g0", "s0", "g1", "s1", "g2", "s2", "g3", "s3", "a0", "a1", "a2", "a3", "a0", "a1", "a2", "a3", "a0", "a1", "a2", "a3", "a0", "a1", "a2", "a3", "a0", "a1", "a2", "a3", "a0", "a1", "a2", "a3", "f0", "f1", "f2", "f3")
BESIDE = ()


def staged(texts):
    reached = [0] * len(CHUNKS)
    out = []
    for text in texts:
        steps = []
        for word in text:
            c = int(word[1:])
            steps.append((word[0], c, reached[c]))
            reached[c] += word[0] == "a"
        out.append(steps)
    assert reached == [6] * len(CHUNKS)
    return out


def place():
    row, grp = lax.axis_index("row"), lax.axis_index("grp")
    return {"core": row % 2, "x": row // 2 % 4, "z": row // 8, "y": grp}


def device(where, **other):
    at = dict(where, **other)
    return ((at["z"] * 4 + at["x"]) * 2 + at["core"], at["y"])


def spot(block):
    index = UPPER.index(block)
    chunk = max(c for c in range(len(CHUNKS)) if FIRST[c] <= index)
    stack, col = divmod(index - FIRST[chunk], CHUNKS[chunk][0] // STACKS)
    return chunk, pl.ds(stack * BLOCK, BLOCK), pl.ds(col * BLOCK, BLOCK)


def offset(value):
    return pl.multiple_of(value, 8)


class Sum:
    def __init__(self, chunk, refs, send_sem, recv_sem, me):
        order = CHUNKS[chunk][1]
        self.part, self.near, self.slots, self.full = refs[0], refs[1], refs[2:5], refs[5]
        self.order, self.chunk, self.send_sem, self.recv_sem, self.me = order, chunk, send_sem, recv_sem, me
        self.half = self.part.shape[0] // 2
        self.own = offset(me["core"] * self.half)
        self.m1 = self.half // SIZES[order[0]]
        self.m2 = self.m1 // SIZES[order[1]]
        self.base1 = offset(self.own + me[order[0]] * self.m1)
        self.base2 = offset(self.base1 + me[order[1]] * self.m2)

    def copy(self, src, dst, stage, k, peer):
        return pltpu.make_async_remote_copy(
            src_ref=src, dst_ref=dst, send_sem=self.send_sem.at[self.chunk, stage, k],
            recv_sem=self.recv_sem.at[self.chunk, stage, k], device_id=peer, device_id_type=MESH)

    def peers(self, axis):
        size = SIZES[axis]
        there = [(self.me[axis] + off) % size for off in range(1, size)]
        return [(k, t, device(self.me, **{axis: t})) for k, t in enumerate(there)]

    def copies(self, stage):
        part, full, order = self.part, self.full, self.order
        if stage in (0, 6):
            partner = device(self.me, core=1 - self.me["core"])
            if stage == 0:
                other = offset((1 - self.me["core"]) * self.half)
                return [self.copy(part.at[pl.ds(other, self.half)], self.near, stage, 0, partner)]
            piece = full.at[pl.ds(self.own, self.half)]
            return [self.copy(piece, piece, stage, 0, partner)]
        axis = order[{1: 0, 2: 1, 3: 2, 4: 1, 5: 0}[stage]]
        out = []
        for k, t, peer in self.peers(axis):
            if stage == 1:
                src, dst = part.at[pl.ds(offset(self.own + t * self.m1), self.m1)], self.slots[0].at[k]
            elif stage == 2:
                src, dst = part.at[pl.ds(offset(self.base1 + t * self.m2), self.m2)], self.slots[1].at[k]
            elif stage == 3:
                src, dst = part.at[pl.ds(self.base2, self.m2)], self.slots[2].at[k]
            else:
                at, m = (self.base2, self.m2) if stage == 4 else (self.base1, self.m1)
                src = dst = full.at[pl.ds(at, m)]
            out.append(self.copy(src, dst, stage, k, peer))
        return out

    def start(self, stage):
        for c in self.copies(stage):
            c.start()

    def finish(self, stage):
        for c in self.copies(stage):
            c.wait()

    def advance(self, stage):
        self.finish(stage)
        part = self.part
        if stage == 0:
            part[pl.ds(self.own, self.half)] = part[pl.ds(self.own, self.half)] + self.near[...]
        elif stage < 4:
            at, m = (self.base1, self.m1) if stage == 1 else (self.base2, self.m2)
            total = part[pl.ds(at, m)]
            slots = self.slots[stage - 1]
            for k in range(slots.shape[0]):
                total = total + slots[k]
            into = self.full if stage == 3 else part
            into[pl.ds(at, m)] = total
        self.start(stage + 1)


def buffers(blocks, order):
    rows, cols = STACKS * BLOCK, blocks // STACKS * BLOCK
    half = rows // 2
    m1 = half // SIZES[order[0]]
    m2 = m1 // SIZES[order[1]]
    shapes = [(rows, cols), (half, cols), (SIZES[order[0]] - 1, m1, cols), (SIZES[order[1]] - 1, m2, cols),
              (SIZES[order[2]] - 1, m2, cols), (rows, cols)]
    return [pltpu.VMEM(shape, jnp.float32) for shape in shapes]


def hadamard_list(size):
    return [[1 - 2 * ((i & k).bit_count() % 2) for k in range(size)] for i in range(size)]


def lane(x, l):
    return jnp.broadcast_to(x[:, l:l + 1], (8, BLOCK))


def invert_factor(rows, midway):
    groups = len(rows)
    lanes = lax.broadcasted_iota(jnp.int32, (8, BLOCK), 1)
    subs = lax.broadcasted_iota(jnp.int32, (8, BLOCK), 0)
    rows = list(rows)
    for b in range(groups):
        if b == groups // 2:
            midway()
        j0 = 8 * b
        here = rows[b]
        row = [jnp.broadcast_to(here[k:k + 1, :], (8, BLOCK)) for k in range(8)]
        s = {(k, l): lane(row[k], j0 + l) for k in range(8) for l in range(k, 8)}
        below = range(b + 1, groups)
        col = {(q, l): lane(rows[q], j0 + l) for q in below for l in range(8)}
        inside = (lanes >= j0) & (lanes < j0 + 8)
        row = [jnp.where(inside, (lanes == j0 + k).astype(jnp.float32), row[k]) for k in range(8)]
        mult = {}
        for k in range(8):
            root = lax.rsqrt(s[k, k])
            row[k] = row[k] * root
            for l in range(k + 1, 8):
                s[k, l] = s[k, l] * root
            for i in range(k + 1, 8):
                for l in range(i, 8):
                    s[i, l] = s[i, l] - s[k, i] * s[k, l]
                row[i] = row[i] - s[k, i] * row[k]
            for q in below:
                m = col[q, k] * root
                mult[q, k] = m
                for l in range(k + 1, 8):
                    col[q, l] = col[q, l] - m * s[k, l]
        for q in below:
            acc = jnp.where(inside, 0.0, rows[q])
            for k in range(8):
                acc = acc - mult[q, k] * row[k]
            rows[q] = acc
        out = row[0]
        for k in range(1, 8):
            out = jnp.where(subs == k, row[k], out)
        rows[b] = jnp.where(lanes <= subs + j0, out, 0.0)
    return rows


def factor_kernel(panel_ref, sign_ref, ids_ref, o_ref, table, mixed, mid_y, mid_r, got, keep, sketch, a,
                  swap_sem, send_sem, recv_sem, *chunk_refs):
    me = place()
    n_dev = got.shape[0] * got.shape[1]
    rows_dev, n_cols = panel_ref.shape
    n_row, n_grp, n_chip = got.shape[0], got.shape[1], got.shape[0] // 2
    my_row, my_grp, core = (me["z"] * SIZES["x"] + me["x"]) * 2 + me["core"], me["y"], me["core"]
    my_chip = my_row // 2
    half = rows_dev // 2

    barrier = pltpu.get_barrier_semaphore()

    def next_chip(off):
        return (my_chip + off) % n_chip

    def greet(row, grp):
        pl.semaphore_signal(barrier, inc=1, device_id=(row, grp), device_id_type=MESH)

    for off in range(1, n_grp):
        greet(my_row, (my_grp + off) % n_grp)
    greet(my_row + 1 - 2 * core, my_grp)

    @pl.loop(1, n_chip)
    def _(off):
        greet(2 * next_chip(off), my_grp)
        greet(2 * next_chip(off) + 1, my_grp)

    base = hadamard(BLOCK, jnp.float32)
    corner = hadamard_list(rows_dev // BLOCK)
    flip = (1 - 2 * sign_ref[...]).astype(jnp.float32)
    for i, signs in enumerate(corner):
        for k, sign in enumerate(signs):
            table[i * BLOCK:(i + 1) * BLOCK, k * BLOCK:(k + 1) * BLOCK] = (base * sign).astype(jnp.bfloat16)
    flat = mixed.reshape(rows_dev * 8, BLOCK)

    def mix(h):
        signed = (table[h * half:(h + 1) * half, :].astype(jnp.float32) * flip).astype(jnp.bfloat16)
        part = jnp.dot(signed, panel_ref[...], preferred_element_type=jnp.float32)
        for k in range(8):
            flat[pl.ds(h * half * 8 + k, half, 8), :] = part[:, k * BLOCK:(k + 1) * BLOCK]

    def remote(src, dst, sem, row, grp):
        return pltpu.make_async_remote_copy(
            src_ref=src, dst_ref=dst, send_sem=swap_sem.at[0, sem], recv_sem=swap_sem.at[1, sem],
            device_id=(row, grp), device_id_type=MESH)

    def here(src, dst, sem):
        return pltpu.make_async_copy(src, dst, swap_sem.at[0, sem])

    def waits(sent, received, sem):
        if sent is not None:
            remote(sent, sent, sem, my_row, my_grp).wait_send()
        if received is not None:
            remote(received, received, sem, my_row, my_grp).wait_recv()

    mix(0)
    pl.semaphore_wait(barrier, n_row + n_grp - 2)
    per_grp = half // n_grp
    for off in range(1, n_grp):
        t = (my_grp + off) % n_grp
        remote(mixed.at[pl.ds(t * per_grp, per_grp)], mid_y.at[my_grp], off, my_row, t).start()
    own_y = here(mixed.at[pl.ds(my_grp * per_grp, per_grp)], mid_y.at[my_grp], 8)
    own_y.start()
    mix(1)

    def to_second(chip):
        return remote(mixed.at[pl.ds(half + chip * n_grp, n_grp)], mid_r.at[my_row], 0, 2 * chip + 1, my_grp)

    own_r = here(mixed.at[pl.ds(half + my_chip * n_grp, n_grp)], mid_r.at[my_row], 9)

    @pl.loop(1, n_chip)
    def _(off):
        to_second(next_chip(off)).start()

    @pl.when(core == 0)
    def _():
        to_second(my_chip).start()

    @pl.when(core == 1)
    def _():
        own_r.start()

    position = jnp.where(core == 0, my_grp * n_chip + my_chip, half + my_chip * n_grp + my_grp)
    wanted = lax.broadcasted_iota(jnp.int32, (n_dev, BLOCK), 0) * rows_dev + position
    hits = jnp.zeros((n_dev, BLOCK), jnp.int32)
    for i in range(ids_ref.shape[0]):
        hits = jnp.where(ids_ref[i:i + 1, :] == wanted, 1, hits)
    norm_scale = 1.0 / math.sqrt(rows_dev * n_dev * ids_ref.shape[0] * ids_ref.shape[1])
    keep[...] = jnp.max(hits, axis=1, keepdims=True).astype(jnp.float32) * norm_scale

    for off in range(1, n_grp):
        remote(mid_y.at[0], mid_y.at[0], off, my_row, my_grp).wait()
    own_y.wait()

    def to_first(chip):
        return remote(mid_y.at[:, chip], got.at[my_row], 10, 2 * chip, my_grp)

    own_f = here(mid_y.at[:, my_chip], got.at[my_row], 11)

    @pl.loop(1, n_chip)
    def _(off):
        to_first(next_chip(off)).start()

    @pl.when(core == 1)
    def _():
        to_first(my_chip).start()
        own_r.wait()
        waits(mid_r.at[pl.ds(0, n_chip - 1)], mid_r.at[pl.ds(0, n_row - 1)], 0)
        for off in range(1, n_grp):
            t = (my_grp + off) % n_grp
            remote(mid_r.at[:, t], got.at[:, my_grp], 11 + off, my_row, t).start()
        own_g = here(mid_r.at[:, my_grp], got.at[:, my_grp], 11)
        own_g.start()
        waits(got.at[pl.ds(0, n_chip)], None, 10)
        for off in range(1, n_grp):
            remote(got.at[:, 0], got.at[:, 0], 11 + off, my_row, my_grp).wait()
        own_g.wait()

    @pl.when(core == 0)
    def _():
        own_f.start()
        waits(mid_r.at[pl.ds(0, n_chip)], None, 0)
        waits(got.at[pl.ds(0, n_chip - 1)], got.at[pl.ds(0, n_row - 1)], 10)
        own_f.wait()

    flat_got = got.reshape(n_dev * 8, BLOCK)
    for k in range(0, 8, 2):
        rest = jnp.concatenate([flat_got[pl.ds(k, n_dev, 8), :], flat_got[pl.ds(k + 1, n_dev, 8), :]], axis=1)
        total = jnp.zeros_like(rest)
        for _ in range(3):
            top = rest.astype(jnp.bfloat16)
            total = total + jnp.dot(table[...], top, preferred_element_type=jnp.float32)
            rest = rest - top.astype(jnp.float32)
        sketch[:, k * BLOCK:(k + 2) * BLOCK] = (total * keep[...]).astype(jnp.bfloat16)

    per = len(chunk_refs) // len(CHUNKS)
    sums = [Sum(c, chunk_refs[per * c:per * c + per], send_sem, recv_sem, me) for c in range(len(CHUNKS))]

    def gram(c):
        blocks = UPPER[FIRST[c]:FIRST[c] + CHUNKS[c][0]]
        for i in sorted({i for i, _ in blocks}):
            ks = [k for bi, k in blocks if bi == i]
            wide = lax.dot_general(
                sketch[:, i * BLOCK:(i + 1) * BLOCK], sketch[:, ks[0] * BLOCK:(ks[-1] + 1) * BLOCK],
                (((0,), (0,)), ((), ())), preferred_element_type=jnp.float32)
            for n, k in enumerate(ks):
                _, rows, cols = spot((i, k))
                sums[c].part[rows, cols] = wide[:, n * BLOCK:(n + 1) * BLOCK]

    def run(steps):
        for what, c, stage in steps:
            if what == "g":
                gram(c)
            elif what == "s":
                sums[c].start(stage)
            elif what == "a":
                sums[c].advance(stage)
            else:
                sums[c].finish(stage)

    before, *beside = staged((BEFORE, *BESIDE))
    run(before)

    out_rows = o_ref.shape[0]
    o_ref[...] = jnp.zeros_like(o_ref)

    def place_block(i, k):
        chunk, rows, cols = spot((i, k))
        a[i * BLOCK:(i + 1) * BLOCK, k * BLOCK:(k + 1) * BLOCK] = sums[chunk].full[rows, cols]

    def updated(t, first):
        lo, col = BLOCK * t, BLOCK * first
        a[lo:lo + BLOCK, col:] = a[lo:lo + BLOCK, col:] - jnp.dot(
            a[lo:lo + BLOCK, :lo], a[:lo, col:], precision=HIGHEST, preferred_element_type=jnp.float32)

    place_block(0, 0)

    @pl.loop(0, N_BLOCKS)
    def _(j):
        for t in range(1, N_BLOCKS):
            @pl.when(j == t)
            def _():
                for k in range(t, N_BLOCKS):
                    place_block(t, k)
                updated(t, t)

        base = pl.multiple_of(j * BLOCK, BLOCK)
        rows = [a[pl.ds(base + 8 * q, 8), pl.ds(base, BLOCK)] for q in range(BLOCK // 8)]

        def midway():
            for t, steps in enumerate(beside[0::2]):
                @pl.when(j == t)
                def _():
                    run(steps)

        inverse = jnp.concatenate(invert_factor(rows, midway), axis=0)
        for t in range(N_BLOCKS):
            @pl.when(j == t)
            def _():
                lo = BLOCK * t
                if t == 0:
                    for k in range(1, N_BLOCKS):
                        place_block(0, k)
                upper = jnp.dot(inverse, a[lo:lo + BLOCK, lo:], precision=HIGHEST, preferred_element_type=jnp.float32)
                a[lo:lo + BLOCK, lo:] = upper
                a[lo:, lo:lo + BLOCK] = upper.T

                @pl.when((my_grp == t) & (my_row * out_rows >= lo))
                def _():
                    first = offset(my_row * out_rows)
                    mine = a[pl.ds(first, out_rows), lo:lo + BLOCK]
                    r = lax.broadcasted_iota(jnp.int32, mine.shape, 0) + first
                    c = lax.broadcasted_iota(jnp.int32, mine.shape, 1) + lo
                    o_ref[...] = jnp.where(r >= c, mine, 0.0)

                if 2 * t + 1 < len(beside):
                    run(beside[2 * t + 1])


def factor_share(panel_rows, signs, ids, n_row, n_grp):
    rows_dev, n_cols = panel_rows.shape
    tile = (n_cols // BLOCK, BLOCK)
    scratch = [
        pltpu.VMEM((rows_dev, rows_dev), jnp.bfloat16),
        pltpu.VMEM((rows_dev, *tile), jnp.float32),
        pltpu.VMEM((n_grp, n_row // 2, *tile), jnp.float32),
        pltpu.VMEM((n_row, n_grp, *tile), jnp.float32),
        pltpu.VMEM((n_row, n_grp, *tile), jnp.float32),
        pltpu.VMEM((n_row * n_grp, 1), jnp.float32),
        pltpu.VMEM((n_row * n_grp, n_cols), jnp.bfloat16),
        pltpu.VMEM((n_cols, n_cols), jnp.float32),
        pltpu.SemaphoreType.DMA((2, 19)),
    ]
    scratch += [pltpu.SemaphoreType.DMA((len(CHUNKS), 7, 7))] * 2
    for blocks, order in CHUNKS:
        scratch += buffers(blocks, order)
    return pl.pallas_call(
        factor_kernel,
        out_shape=jax.ShapeDtypeStruct((n_cols // n_row, n_cols // n_grp), jnp.float32),
        in_specs=[pl.BlockSpec(memory_space=pltpu.VMEM)] * 3,
        out_specs=pl.BlockSpec(memory_space=pltpu.VMEM),
        scratch_shapes=scratch,
        compiler_params=pltpu.CompilerParams(collective_id=0, has_side_effects=True, vmem_limit_bytes=VMEM_LIMIT),
        name="factor",
    )(panel_rows, signs, ids)


def local(panel_rows, sign_bits, sample_rows):
    return factor_share(panel_rows, sign_bits[None, :], sample_rows.reshape(-1, BLOCK),
                        lax.axis_size("row"), lax.axis_size("grp"))


def solution(mesh):
    return jax.shard_map(
        local,
        mesh=mesh,
        in_specs=(P(("row", "grp"), None), P(("row", "grp")), P()),
        out_specs=P("row", "grp"),
        check_vma=False,
    )
```

```python
import math

import jax
import jax.numpy as jnp
from jax import lax
from jax.experimental import pallas as pl
from jax.experimental.pallas import tpu as pltpu
from jax.sharding import PartitionSpec as P

HIGHEST = lax.Precision.HIGHEST
MESH = pl.DeviceIdType.MESH
BLOCK = 128
VMEM_LIMIT = 48 * 2**20


def hadamard(table_size, dtype):
    row_ids = lax.broadcasted_iota(jnp.int32, (table_size, table_size), 0)
    col_ids = lax.broadcasted_iota(jnp.int32, (table_size, table_size), 1)
    shared = row_ids & col_ids
    parity = jnp.zeros((table_size, table_size), jnp.int32)
    for bit_pos in range(table_size.bit_length() - 1):
        parity = parity ^ shared >> bit_pos & 1
    return (1 - 2 * parity).astype(dtype)


SIZES = {"x": 4, "y": 8, "z": 8}
STACKS = 4
N_BLOCKS = 8
UPPER = [(i, k) for i in range(N_BLOCKS) for k in range(i, N_BLOCKS)]
CHUNKS = ((12, "xyz"), (8, "xzy"), (8, "yxz"), (8, "zxy"))
FIRST = [sum(n for n, _ in CHUNKS[:c]) for c in range(len(CHUNKS))]
BEFORE = ("g0", "s0", "g1", "s1", "g2", "s2", "g3", "s3", "a0", "a1", "a2", "a3", "a0", "a1", "a2", "a3", "a0", "a1", "a2", "a3", "a0", "a1", "a2", "a3", "a0", "a1", "a2", "a3", "a0", "a1", "a2", "a3", "f0", "f1", "f2", "f3")
BESIDE = ()


def staged(texts):
    reached = [0] * len(CHUNKS)
    out = []
    for text in texts:
        steps = []
        for word in text:
            c = int(word[1:])
            steps.append((word[0], c, reached[c]))
            reached[c] += word[0] == "a"
        out.append(steps)
    assert reached == [6] * len(CHUNKS)
    return out


def place():
    row, grp = lax.axis_index("row"), lax.axis_index("grp")
    return {"core": row % 2, "x": row // 2 % 4, "z": row // 8, "y": grp}


def device(where, **other):
    at = dict(where, **other)
    return ((at["z"] * 4 + at["x"]) * 2 + at["core"], at["y"])


def spot(block):
    index = UPPER.index(block)
    chunk = max(c for c in range(len(CHUNKS)) if FIRST[c] <= index)
    stack, col = divmod(index - FIRST[chunk], CHUNKS[chunk][0] // STACKS)
    return chunk, pl.ds(stack * BLOCK, BLOCK), pl.ds(col * BLOCK, BLOCK)


def offset(value):
    return pl.multiple_of(value, 8)


class Sum:
    def __init__(self, chunk, refs, send_sem, recv_sem, me):
        order = CHUNKS[chunk][1]
        self.part, self.near, self.slots, self.full = refs[0], refs[1], refs[2:5], refs[5]
        self.order, self.chunk, self.send_sem, self.recv_sem, self.me = order, chunk, send_sem, recv_sem, me
        self.half = self.part.shape[0] // 2
        self.own = offset(me["core"] * self.half)
        self.m1 = self.half // SIZES[order[0]]
        self.m2 = self.m1 // SIZES[order[1]]
        self.base1 = offset(self.own + me[order[0]] * self.m1)
        self.base2 = offset(self.base1 + me[order[1]] * self.m2)

    def copy(self, src, dst, stage, k, peer):
        return pltpu.make_async_remote_copy(
            src_ref=src, dst_ref=dst, send_sem=self.send_sem.at[self.chunk, stage, k],
            recv_sem=self.recv_sem.at[self.chunk, stage, k], device_id=peer, device_id_type=MESH)

    def peers(self, axis):
        size = SIZES[axis]
        there = [(self.me[axis] + off) % size for off in range(1, size)]
        return [(k, t, device(self.me, **{axis: t})) for k, t in enumerate(there)]

    def copies(self, stage):
        part, full, order = self.part, self.full, self.order
        if stage in (0, 6):
            partner = device(self.me, core=1 - self.me["core"])
            if stage == 0:
                other = offset((1 - self.me["core"]) * self.half)
                return [self.copy(part.at[pl.ds(other, self.half)], self.near, stage, 0, partner)]
            piece = full.at[pl.ds(self.own, self.half)]
            return [self.copy(piece, piece, stage, 0, partner)]
        axis = order[{1: 0, 2: 1, 3: 2, 4: 1, 5: 0}[stage]]
        out = []
        for k, t, peer in self.peers(axis):
            if stage == 1:
                src, dst = part.at[pl.ds(offset(self.own + t * self.m1), self.m1)], self.slots[0].at[k]
            elif stage == 2:
                src, dst = part.at[pl.ds(offset(self.base1 + t * self.m2), self.m2)], self.slots[1].at[k]
            elif stage == 3:
                src, dst = part.at[pl.ds(self.base2, self.m2)], self.slots[2].at[k]
            else:
                at, m = (self.base2, self.m2) if stage == 4 else (self.base1, self.m1)
                src = dst = full.at[pl.ds(at, m)]
            out.append(self.copy(src, dst, stage, k, peer))
        return out

    def start(self, stage):
        for c in self.copies(stage):
            c.start()

    def finish(self, stage):
        for c in self.copies(stage):
            c.wait()

    def advance(self, stage):
        self.finish(stage)
        part = self.part
        if stage == 0:
            part[pl.ds(self.own, self.half)] = part[pl.ds(self.own, self.half)] + self.near[...]
        elif stage < 4:
            at, m = (self.base1, self.m1) if stage == 1 else (self.base2, self.m2)
            total = part[pl.ds(at, m)]
            slots = self.slots[stage - 1]
            for k in range(slots.shape[0]):
                total = total + slots[k]
            into = self.full if stage == 3 else part
            into[pl.ds(at, m)] = total
        self.start(stage + 1)


def buffers(blocks, order):
    rows, cols = STACKS * BLOCK, blocks // STACKS * BLOCK
    half = rows // 2
    m1 = half // SIZES[order[0]]
    m2 = m1 // SIZES[order[1]]
    shapes = [(rows, cols), (half, cols), (SIZES[order[0]] - 1, m1, cols), (SIZES[order[1]] - 1, m2, cols),
              (SIZES[order[2]] - 1, m2, cols), (rows, cols)]
    return [pltpu.VMEM(shape, jnp.float32) for shape in shapes]


def hadamard_list(size):
    return [[1 - 2 * ((i & k).bit_count() % 2) for k in range(size)] for i in range(size)]


SPAN = 4


def dot_split(left, right):
    def parts(x):
        high = x.astype(jnp.bfloat16)
        rest = x - high.astype(jnp.float32)
        mid = rest.astype(jnp.bfloat16)
        return high, mid, (rest - mid.astype(jnp.float32)).astype(jnp.bfloat16)
    h, m, l = parts(left)
    hh, mm, ll = parts(right)
    return lax.dot_general(
        jnp.concatenate([h, h, m, h, l, m], 0), jnp.concatenate([hh, mm, hh, ll, hh, mm], 0),
        (((0,), (0,)), ((), ())), preferred_element_type=jnp.float32)


def lane(x, l):
    return jnp.broadcast_to(x[:, l:l + 1], (8, BLOCK))


def invert_factor(rows, midway):
    groups = len(rows)
    lanes = lax.broadcasted_iota(jnp.int32, (8, BLOCK), 1)
    subs = lax.broadcasted_iota(jnp.int32, (8, BLOCK), 0)
    rows = list(rows)
    for b in range(groups):
        if b == groups // 2:
            midway()
        j0 = 8 * b
        start = b - b % SPAN
        here = rows[b]
        row = [jnp.broadcast_to(here[k:k + 1, :], (8, BLOCK)) for k in range(8)]
        s = {(k, l): lane(row[k], j0 + l) for k in range(8) for l in range(k, 8)}
        below = range(b + 1, start + SPAN)
        col = {(q, l): lane(rows[q], j0 + l) for q in below for l in range(8)}
        inside = (lanes >= j0) & (lanes < j0 + 8)
        row = [jnp.where(inside, (lanes == j0 + k).astype(jnp.float32), row[k]) for k in range(8)]
        mult = {}
        for k in range(8):
            root = lax.rsqrt(s[k, k])
            row[k] = row[k] * root
            for l in range(k + 1, 8):
                s[k, l] = s[k, l] * root
            for i in range(k + 1, 8):
                for l in range(i, 8):
                    s[i, l] = s[i, l] - s[k, i] * s[k, l]
                row[i] = row[i] - s[k, i] * row[k]
            for q in below:
                m = col[q, k] * root
                mult[q, k] = m
                for l in range(k + 1, 8):
                    col[q, l] = col[q, l] - m * s[k, l]
        for q in below:
            acc = jnp.where(inside, 0.0, rows[q])
            for k in range(8):
                acc = acc - mult[q, k] * row[k]
            rows[q] = acc
        out = row[0]
        for k in range(1, 8):
            out = jnp.where(subs == k, row[k], out)
        rows[b] = out
        if b + 1 == start + SPAN:
            low, high = 8 * start, 8 * (b + 1)
            whole = jnp.concatenate(rows[start:b + 1], axis=0)
            place_row = lax.broadcasted_iota(jnp.int32, whole.shape, 0) + low
            place_col = lax.broadcasted_iota(jnp.int32, whole.shape, 1)
            solved = jnp.where((place_col > place_row) & (place_col < high), 0.0, whole)
            for q in range(start, b + 1):
                rows[q] = jnp.where(lanes <= subs + 8 * q, rows[q], 0.0)
            if b + 1 < groups:
                taken = dot_split(whole, solved)
                span_lanes = (lanes >= low) & (lanes < high)
                for q in range(b + 1, groups):
                    rows[q] = jnp.where(span_lanes, 0.0, rows[q]) - taken[8 * q:8 * q + 8]
    return rows


def factor_kernel(panel_in, sign_ref, ids_ref, o_ref, panel_ref, panel_sem, table, mixed, mid_y, mid_r, got, keep, sketch, a,
                  swap_sem, send_sem, recv_sem, *chunk_refs):
    me = place()
    n_dev = got.shape[0] * got.shape[1]
    rows_dev, n_cols = panel_in.shape
    n_row, n_grp, n_chip = got.shape[0], got.shape[1], got.shape[0] // 2
    my_row, my_grp, core = (me["z"] * SIZES["x"] + me["x"]) * 2 + me["core"], me["y"], me["core"]
    my_chip = my_row // 2
    half = rows_dev // 2

    barrier = pltpu.get_barrier_semaphore()
    fetch = pltpu.make_async_copy(panel_in, panel_ref, panel_sem)
    fetch.start()

    def next_chip(off):
        return (my_chip + off) % n_chip

    def greet(row, grp):
        pl.semaphore_signal(barrier, inc=1, device_id=(row, grp), device_id_type=MESH)

    for off in range(1, n_grp):
        greet(my_row, (my_grp + off) % n_grp)
    greet(my_row + 1 - 2 * core, my_grp)

    @pl.loop(1, n_chip)
    def _(off):
        greet(2 * next_chip(off), my_grp)
        greet(2 * next_chip(off) + 1, my_grp)

    base = hadamard(BLOCK, jnp.float32)
    corner = hadamard_list(rows_dev // BLOCK)
    flip = (1 - 2 * sign_ref[...]).astype(jnp.float32)
    for i, signs in enumerate(corner):
        for k, sign in enumerate(signs):
            table[i * BLOCK:(i + 1) * BLOCK, k * BLOCK:(k + 1) * BLOCK] = (base * sign).astype(jnp.bfloat16)
    flat = mixed.reshape(rows_dev * 8, BLOCK)

    def mix(h):
        signed = (table[h * half:(h + 1) * half, :].astype(jnp.float32) * flip).astype(jnp.bfloat16)
        part = jnp.dot(signed, panel_ref[...], preferred_element_type=jnp.float32)
        for k in range(8):
            flat[pl.ds(h * half * 8 + k, half, 8), :] = part[:, k * BLOCK:(k + 1) * BLOCK]

    def remote(src, dst, sem, row, grp):
        return pltpu.make_async_remote_copy(
            src_ref=src, dst_ref=dst, send_sem=swap_sem.at[0, sem], recv_sem=swap_sem.at[1, sem],
            device_id=(row, grp), device_id_type=MESH)

    def here(src, dst, sem):
        return pltpu.make_async_copy(src, dst, swap_sem.at[0, sem])

    def waits(sent, received, sem):
        if sent is not None:
            remote(sent, sent, sem, my_row, my_grp).wait_send()
        if received is not None:
            remote(received, received, sem, my_row, my_grp).wait_recv()

    fetch.wait()
    mix(0)
    pl.semaphore_wait(barrier, n_row + n_grp - 2)
    per_grp = half // n_grp
    for off in range(1, n_grp):
        t = (my_grp + off) % n_grp
        remote(mixed.at[pl.ds(t * per_grp, per_grp)], mid_y.at[my_grp], off, my_row, t).start()
    own_y = here(mixed.at[pl.ds(my_grp * per_grp, per_grp)], mid_y.at[my_grp], 8)
    own_y.start()
    mix(1)

    def to_second(chip):
        return remote(mixed.at[pl.ds(half + chip * n_grp, n_grp)], mid_r.at[my_row], 0, 2 * chip + 1, my_grp)

    own_r = here(mixed.at[pl.ds(half + my_chip * n_grp, n_grp)], mid_r.at[my_row], 9)

    @pl.loop(1, n_chip)
    def _(off):
        to_second(next_chip(off)).start()

    @pl.when(core == 0)
    def _():
        to_second(my_chip).start()

    @pl.when(core == 1)
    def _():
        own_r.start()

    position = jnp.where(core == 0, my_grp * n_chip + my_chip, half + my_chip * n_grp + my_grp)
    wanted = lax.broadcasted_iota(jnp.int32, (n_dev, BLOCK), 0) * rows_dev + position
    hits = jnp.zeros((n_dev, BLOCK), jnp.int32)
    for i in range(ids_ref.shape[0]):
        hits = jnp.where(ids_ref[i:i + 1, :] == wanted, 1, hits)
    norm_scale = 1.0 / math.sqrt(rows_dev * n_dev * ids_ref.shape[0] * ids_ref.shape[1])
    keep[...] = jnp.max(hits, axis=1, keepdims=True).astype(jnp.float32) * norm_scale

    for off in range(1, n_grp):
        remote(mid_y.at[0], mid_y.at[0], off, my_row, my_grp).wait()
    own_y.wait()

    def to_first(chip):
        return remote(mid_y.at[:, chip], got.at[my_row], 10, 2 * chip, my_grp)

    own_f = here(mid_y.at[:, my_chip], got.at[my_row], 11)

    @pl.loop(1, n_chip)
    def _(off):
        to_first(next_chip(off)).start()

    @pl.when(core == 1)
    def _():
        to_first(my_chip).start()
        own_r.wait()
        waits(mid_r.at[pl.ds(0, n_chip - 1)], mid_r.at[pl.ds(0, n_row - 1)], 0)
        for off in range(1, n_grp):
            t = (my_grp + off) % n_grp
            remote(mid_r.at[:, t], got.at[:, my_grp], 11 + off, my_row, t).start()
        own_g = here(mid_r.at[:, my_grp], got.at[:, my_grp], 11)
        own_g.start()
        waits(got.at[pl.ds(0, n_chip)], None, 10)
        for off in range(1, n_grp):
            remote(got.at[:, 0], got.at[:, 0], 11 + off, my_row, my_grp).wait()
        own_g.wait()

    @pl.when(core == 0)
    def _():
        own_f.start()
        waits(mid_r.at[pl.ds(0, n_chip)], None, 0)
        waits(got.at[pl.ds(0, n_chip - 1)], got.at[pl.ds(0, n_row - 1)], 10)
        own_f.wait()

    flat_got = got.reshape(n_dev * 8, BLOCK)
    for k in range(0, 8, 2):
        rest = jnp.concatenate([flat_got[pl.ds(k, n_dev, 8), :], flat_got[pl.ds(k + 1, n_dev, 8), :]], axis=1)
        total = jnp.zeros_like(rest)
        for _ in range(3):
            top = rest.astype(jnp.bfloat16)
            total = total + jnp.dot(table[...], top, preferred_element_type=jnp.float32)
            rest = rest - top.astype(jnp.float32)
        sketch[:, k * BLOCK:(k + 2) * BLOCK] = (total * keep[...]).astype(jnp.bfloat16)

    per = len(chunk_refs) // len(CHUNKS)
    sums = [Sum(c, chunk_refs[per * c:per * c + per], send_sem, recv_sem, me) for c in range(len(CHUNKS))]

    def gram(c):
        blocks = UPPER[FIRST[c]:FIRST[c] + CHUNKS[c][0]]
        for i in sorted({i for i, _ in blocks}):
            ks = [k for bi, k in blocks if bi == i]
            wide = lax.dot_general(
                sketch[:, i * BLOCK:(i + 1) * BLOCK], sketch[:, ks[0] * BLOCK:(ks[-1] + 1) * BLOCK],
                (((0,), (0,)), ((), ())), preferred_element_type=jnp.float32)
            for n, k in enumerate(ks):
                _, rows, cols = spot((i, k))
                sums[c].part[rows, cols] = wide[:, n * BLOCK:(n + 1) * BLOCK]

    def run(steps):
        for what, c, stage in steps:
            if what == "g":
                gram(c)
            elif what == "s":
                sums[c].start(stage)
            elif what == "a":
                sums[c].advance(stage)
            else:
                sums[c].finish(stage)

    before, *beside = staged((BEFORE, *BESIDE))
    run(before)

    out_rows = o_ref.shape[0]
    o_ref[...] = jnp.zeros_like(o_ref)

    def place_block(i, k):
        chunk, rows, cols = spot((i, k))
        a[i * BLOCK:(i + 1) * BLOCK, k * BLOCK:(k + 1) * BLOCK] = sums[chunk].full[rows, cols]

    def updated(t, first):
        lo, col = BLOCK * t, BLOCK * first
        a[lo:lo + BLOCK, col:] = a[lo:lo + BLOCK, col:] - jnp.dot(
            a[lo:lo + BLOCK, :lo], a[:lo, col:], precision=HIGHEST, preferred_element_type=jnp.float32)

    place_block(0, 0)

    @pl.loop(0, N_BLOCKS)
    def _(j):
        for t in range(1, N_BLOCKS):
            @pl.when(j == t)
            def _():
                for k in range(t, N_BLOCKS):
                    place_block(t, k)
                updated(t, t)

        base = pl.multiple_of(j * BLOCK, BLOCK)
        rows = [a[pl.ds(base + 8 * q, 8), pl.ds(base, BLOCK)] for q in range(BLOCK // 8)]

        def midway():
            for t, steps in enumerate(beside[0::2]):
                @pl.when(j == t)
                def _():
                    run(steps)

        inverse = jnp.concatenate(invert_factor(rows, midway), axis=0)
        for t in range(N_BLOCKS):
            @pl.when(j == t)
            def _():
                lo = BLOCK * t
                if t == 0:
                    for k in range(1, N_BLOCKS):
                        place_block(0, k)
                upper = jnp.dot(inverse, a[lo:lo + BLOCK, lo:], precision=HIGHEST, preferred_element_type=jnp.float32)
                a[lo:lo + BLOCK, lo:] = upper
                a[lo:, lo:lo + BLOCK] = upper.T

                @pl.when((my_grp == t) & (my_row * out_rows >= lo))
                def _():
                    first = offset(my_row * out_rows)
                    mine = a[pl.ds(first, out_rows), lo:lo + BLOCK]
                    r = lax.broadcasted_iota(jnp.int32, mine.shape, 0) + first
                    c = lax.broadcasted_iota(jnp.int32, mine.shape, 1) + lo
                    o_ref[...] = jnp.where(r >= c, mine, 0.0)

                if 2 * t + 1 < len(beside):
                    run(beside[2 * t + 1])


def factor_share(panel_rows, signs, ids, n_row, n_grp):
    rows_dev, n_cols = panel_rows.shape
    tile = (n_cols // BLOCK, BLOCK)
    scratch = [
        pltpu.VMEM(panel_rows.shape, panel_rows.dtype),
        pltpu.SemaphoreType.DMA,
        pltpu.VMEM((rows_dev, rows_dev), jnp.bfloat16),
        pltpu.VMEM((rows_dev, *tile), jnp.float32),
        pltpu.VMEM((n_grp, n_row // 2, *tile), jnp.float32),
        pltpu.VMEM((n_row, n_grp, *tile), jnp.float32),
        pltpu.VMEM((n_row, n_grp, *tile), jnp.float32),
        pltpu.VMEM((n_row * n_grp, 1), jnp.float32),
        pltpu.VMEM((n_row * n_grp, n_cols), jnp.bfloat16),
        pltpu.VMEM((n_cols, n_cols), jnp.float32),
        pltpu.SemaphoreType.DMA((2, 19)),
    ]
    scratch += [pltpu.SemaphoreType.DMA((len(CHUNKS), 7, 7))] * 2
    for blocks, order in CHUNKS:
        scratch += buffers(blocks, order)
    return pl.pallas_call(
        factor_kernel,
        out_shape=jax.ShapeDtypeStruct((n_cols // n_row, n_cols // n_grp), jnp.float32),
        in_specs=[pl.BlockSpec(memory_space=pltpu.HBM)] + [pl.BlockSpec(memory_space=pltpu.VMEM)] * 2,
        out_specs=pl.BlockSpec(memory_space=pltpu.VMEM),
        scratch_shapes=scratch,
        compiler_params=pltpu.CompilerParams(collective_id=0, has_side_effects=True, vmem_limit_bytes=VMEM_LIMIT),
        name="factor",
    )(panel_rows, signs, ids)


def local(panel_rows, sign_bits, sample_rows):
    return factor_share(panel_rows, sign_bits[None, :], sample_rows.reshape(-1, BLOCK),
                        lax.axis_size("row"), lax.axis_size("grp"))


def solution(mesh):
    return jax.shard_map(
        local,
        mesh=mesh,
        in_specs=(P(("row", "grp"), None), P(("row", "grp")), P()),
        out_specs=P("row", "grp"),
        check_vma=False,
    )
```
